32 devices in a mesh: groups: 2 (over x), ctx: 8 (over z, y), tp: 2 (over core).
Axes of the slice: x: 2, y: 2, z: 4, core: 2. Of those that a mesh axis runs over, the one named last changes fastest.
Arguments:
- queries: bfloat16 [3072, 4096], P(('groups', 'ctx'), 'tp'), parts along dimension 0, may hold values from -8 to 8
- keys: bfloat16 [3072, 512], P(('groups', 'ctx'), 'tp'), parts along dimension 0, may hold values from -8 to 8
- values: bfloat16 [3072, 512], P(('groups', 'ctx'), 'tp'), parts along dimension 0, may hold values from -6 to 6
- segments: int32 [3072], P(('groups', 'ctx')), parts along dimension 0, may hold values from 0 to 7, never falling along the last dimension, each value on 1 to 768 neighbouring positions
- valid_length: int32 [2], P('groups'), parts along dimension 0, may hold values from 768 to 1536
- reward_weight: float32 [4096], P('tp'), may hold values from -0.09375 to 0.09375
Outputs:
- attention: bfloat16 [3072, 4096], P(('groups', 'ctx'), 'tp'), parts along dimension 0
- reward: float32 [3072], P(('groups', 'ctx')), parts along dimension 0
The draws below stay inside these ranges and needn't reach their ends.
There are 2 independent parts, one for each index of `groups`. The reference program is written for one: setup_inputs(seed, part) draws one part's arguments, and reference() takes and returns one part's arrays. A program takes and returns all parts, laid end to end along the dimension named above; an argument that names none is the same for every part. Nothing has to cross between parts.
Inputs may be any that keep to these rules, and one draw needn't show every extreme that they name: `segments`: ids never fall along positions; each document spans at most 768 positions.
All inputs are finite; a program needn't handle non-finite values.
Results may differ from the reference program's by a relative error of at most 0.0061.
Values may be sent and summed in bfloat16 or wider, within the bound.
A program may use at most 128 MiB of HBM per device.

```python
import math
import jax
import jax.numpy as jnp
import numpy as np
from jax import lax

HEAD = 128
HEADS = 32
KV_HEADS = 4
TOK_DEV = 192
SEQ = 1536
N_CTX = 8


def draw_keys(key, part):
    key = jax.random.fold_in(key, 11)
    return jnp.clip(jax.random.normal(key, (SEQ, KV_HEADS * HEAD), jnp.float32), -6.0, 6.0).astype(jnp.bfloat16)


def draw_queries(key, part):
    key = jax.random.fold_in(key, 12)
    return jnp.clip(jax.random.normal(key, (SEQ, HEADS * HEAD), jnp.float32), -6.0, 6.0).astype(jnp.bfloat16)


def level_of(key, extent, pieces, least, high):
    factor_of, own = 1.0, jax.random.fold_in(key, 6)
    for axis_at, blocks in pieces:
        steps = jnp.exp(jax.random.uniform(jax.random.fold_in(own, axis_at), (blocks,), jnp.float32, least / len(pieces), high / len(pieces)))
        factor_of = factor_of * jnp.repeat(steps, extent[axis_at] // blocks).reshape([-1 if axis == axis_at else 1 for axis in range(len(extent))])
    return factor_of


def length_profile(number_of, total, reach, lean):
    weights = [(1 << 20) // math.isqrt(rank ** lean) + 1 for rank in range(2, number_of + 1)]
    surplus, given = total - reach - (number_of - 1), [1] * (number_of - 1)
    while surplus > 0:
        movable = [i for i in range(number_of - 1) if given[i] < reach]
        pool, budget = sum([weights[i] for i in movable]), surplus
        for i in movable:
            addition = min(reach - given[i], max(1, budget * weights[i] // pool), surplus)
            given[i] = given[i] + addition
            surplus = surplus - addition
    return np.array([reach] + given)


def uneven(rng, count, total, reach, skew):
    if count == 2:
        one = jax.random.randint(rng, (), max(1, total - reach), min(reach, total - 1) + 1)
        return jnp.stack([one, total - one])
    sizes = jnp.asarray(length_profile(count, total, reach, skew), jnp.int32)
    twos = (count - 1) // 2
    donor, sink = sizes[1:1 + 2 * twos:2], sizes[2:2 + 2 * twos:2]
    margin = jnp.minimum(donor - 1, reach - sink)
    passed = jax.random.randint(jax.random.fold_in(rng, 1), (twos,), 0, 1 << 20) % (margin + 1)
    sizes = sizes.at[1:1 + 2 * twos:2].set(donor - passed).at[2:2 + 2 * twos:2].set(sink + passed)
    return sizes[jax.random.permutation(jax.random.fold_in(rng, 2), count)]


def gaussian(rng, extent, deviation, limit, cuts=(), kind=jnp.bfloat16):
    drawn = jax.random.normal(rng, extent, jnp.float32) * deviation
    if len(cuts) > 0:
        drawn = level_of(rng, extent, cuts, -0.22, 0.18) * drawn
    return jnp.clip(drawn, min=-limit, max=limit).astype(kind)


def setup_inputs(seed: int = 0, part: int = 0) -> dict:
    splits = jax.random.split(jax.random.key(seed), 7)
    part_splits = jax.random.split(jax.random.fold_in(splits[6], part), 7)
    return {
        "queries": draw_queries(jax.random.fold_in(jax.random.fold_in(splits[6], part), 71), part),
        "keys": draw_keys(jax.random.fold_in(jax.random.fold_in(splits[6], part), 71), part),
        "values": gaussian(part_splits[2], (SEQ, KV_HEADS * HEAD), 1.0, 6.0, ((0, 8), (1, 2))),
        "segments": jnp.searchsorted(jnp.cumsum(uneven(part_splits[3], 8, SEQ, SEQ // 2, 1)), jnp.arange(SEQ), side="right").astype(jnp.int32),
        "valid_length": jax.random.randint(part_splits[4], (1,), SEQ // 2, SEQ + 1).astype(jnp.int32),
        "reward_weight": gaussian(splits[5], (HEADS * HEAD,), (HEADS * HEAD) ** -0.5, 0.09375, ((0, 2),), jnp.float32),
    }


def rotate(matrix, positions, heads):
    row_count = matrix.shape[0]
    half_dim = HEAD // 2
    entries = matrix.astype(jnp.float32).reshape(row_count, heads, HEAD)
    steps_index = jnp.arange(half_dim).astype(jnp.float32)
    frequency = jnp.exp(steps_index * (-2.0 * math.log(1000000.0) / HEAD))
    angles = positions.astype(jnp.float32)[:, None] * frequency[None, :]
    cosine = jnp.cos(angles)[:, None, :]
    sine = jnp.sin(angles)[:, None, :]
    lower = entries[..., :half_dim]
    upper = entries[..., half_dim:]
    turned = jnp.concatenate([lower * cosine - upper * sine, upper * cosine + lower * sine], axis=-1)
    return turned.reshape(row_count, heads * HEAD).astype(jnp.bfloat16)


def reference(queries, keys, values, segments, valid_length, reward_weight):
    positions = jnp.arange(SEQ, dtype=jnp.int32)
    q_rot = rotate(queries, positions, HEADS)
    k_rot = rotate(keys, positions, KV_HEADS)
    group_size = HEADS // KV_HEADS
    valid_rows = valid_length[0]
    key_full = k_rot.astype(jnp.float32).reshape(SEQ, KV_HEADS, HEAD)
    value_full = values.astype(jnp.float32).reshape(SEQ, KV_HEADS, HEAD)

    def block_out(index):
        begin_row = (index * TOK_DEV).astype(jnp.int32)
        query_rows = lax.dynamic_slice_in_dim(q_rot, begin_row, TOK_DEV, 0).astype(jnp.float32)
        query_rows = query_rows.reshape(TOK_DEV, KV_HEADS, group_size, HEAD)
        query_pos = begin_row + jnp.arange(TOK_DEV, dtype=jnp.int32)
        query_doc = lax.dynamic_slice_in_dim(segments, begin_row, TOK_DEV, 0)
        scores = jnp.einsum("rkgd,skd->kgrs", query_rows, key_full, precision=lax.Precision.HIGHEST) * (HEAD ** -0.5)
        allowed = (segments[None, :] == query_doc[:, None]) & (positions[None, :] <= query_pos[:, None])
        allowed = allowed & ((positions[None, :] < valid_rows) | (positions[None, :] == query_pos[:, None]))
        masked = jnp.where(allowed, scores, -jnp.inf)
        row_max = jnp.max(masked, axis=-1, keepdims=True)
        weights = jnp.where(allowed, jnp.exp(scores - row_max), 0.0)
        row_sum = jnp.sum(weights, axis=-1)
        rounded = lax.optimization_barrier(weights.astype(jnp.bfloat16)).astype(jnp.float32)
        mixed = jnp.einsum("kgrs,skd->kgrd", rounded, value_full, precision=lax.Precision.HIGHEST)
        normed = mixed / row_sum[..., None]
        flat = jnp.transpose(normed, (2, 0, 1, 3)).reshape(TOK_DEV, HEADS * HEAD)
        return flat * (query_pos < valid_rows).astype(jnp.float32)[:, None]

    outputs = lax.map(block_out, jnp.arange(N_CTX, dtype=jnp.int32)).reshape(SEQ, HEADS * HEAD)
    attention = outputs.astype(jnp.bfloat16)
    reward = jnp.dot(outputs, reward_weight, precision=lax.Precision.HIGHEST)
    return attention, reward
```

```python
import functools
import math

import jax
import jax.numpy as jnp
from jax import lax
from jax.experimental import pallas as pl
from jax.experimental.pallas import tpu as pltpu
from jax.sharding import PartitionSpec as P

HEAD = 128
LANES = 128
MESH = pl.DeviceIdType.MESH
SCALE = HEAD**-0.5 * math.log2(math.e)
BLOCKED = -1e30


def kernel(
    n,
    window,
    ways,
    q_hbm,
    k_ref,
    v_ref,
    seg_ref,
    valid_ref,
    weight_ref,
    out_hbm,
    reward_ref,
    q_in,
    q_rot,
    k_own,
    k_buf,
    v_buf,
    seg_own,
    seg_buf,
    bias_ref,
    max_ref,
    acc_ref,
    out_buf,
    rew_acc,
    rew_own,
    rew_far,
    send_sem,
    recv_sem,
    local_sem,
    rew_sem,
):
    rows = k_ref.shape[0]
    kv_heads = k_ref.shape[1] // HEAD
    q_heads = q_in.shape[1] // HEAD
    group = q_heads // kv_heads
    chunks = 1 + 2 * kv_heads
    me = lax.axis_index("ctx")
    other = 1 - lax.axis_index("tp")
    odd = lax.rem(me, 2)

    load = pltpu.make_async_copy(q_hbm, q_in, local_sem.at[0])
    load.start()

    def outgoing(slot):
        held = me - 1 - slot >= 0
        if ways == 1:
            return [(0, slot + 1, me + 1, held & (me + 1 < n))] if slot + 1 < window else []
        sends = []
        if slot == -1 or slot % 2 == 1:
            if slot + 2 < window:
                sends.append((0, slot + 2, me + 2, held & (me + 2 < n)))
            if slot + 1 < window:
                sends.append((1, slot + 1, me + 1, held & (odd == 0)))
            if slot >= 1:
                sends.append((2, slot - 1, me - 1, held & (odd == 1)))
        return sends

    def piece(slot, chunk):
        if chunk == 0:
            return seg_own if slot < 0 else seg_buf.at[slot]
        head, is_key = (chunk - 1) // 2, (chunk - 1) % 2 == 1
        if slot < 0:
            return k_own.at[head] if is_key else v_ref.at[:, pl.ds(head * HEAD, HEAD)]
        return (k_buf if is_key else v_buf).at[head, pl.ds(slot * rows, rows)]

    def copy_of(slot, chunk, path, there, device):
        return pltpu.make_async_remote_copy(
            src_ref=piece(slot, chunk),
            dst_ref=piece(there, chunk),
            send_sem=send_sem.at[path, there, chunk],
            recv_sem=recv_sem.at[there, chunk],
            device_id={"ctx": device},
            device_id_type=MESH,
        )

    def send(slot, chunk):
        for path, there, device, condition in outgoing(slot):
            @pl.when(condition)
            def _(path=path, there=there, device=device):
                copy_of(slot, chunk, path, there, device).start()

    def finish_send(slot, chunk):
        for path, there, device, condition in outgoing(slot):
            @pl.when(condition)
            def _(path=path, there=there, device=device):
                copy_of(slot, chunk, path, there, device).wait_send()

    def arrive(slot, chunk):
        @pl.when(me - 1 - slot >= 0)
        def _():
            copy_of(slot, chunk, 0, slot, me).wait_recv()

        send(slot, chunk)

    seg_own[...] = jnp.zeros_like(seg_own)
    seg_own[:, :rows] = seg_ref[...]
    for slot in range(window):
        @pl.when(me - 1 - slot < 0)
        def _(slot=slot):
            seg_buf[slot] = jnp.zeros(seg_buf.shape[1:], seg_buf.dtype)
            for head in range(kv_heads):
                k_buf[head, slot * rows : (slot + 1) * rows] = jnp.zeros((rows, HEAD), k_buf.dtype)
                v_buf[head, slot * rows : (slot + 1) * rows] = jnp.zeros((rows, HEAD), v_buf.dtype)

    barrier = pltpu.get_barrier_semaphore()
    pl.semaphore_signal(barrier, inc=1, device_id={"tp": other}, device_id_type=MESH)
    if ways == 2:
        pl.semaphore_signal(barrier, inc=1, device_id={"ctx": me + 1 - 2 * odd}, device_id_type=MESH)

    @pl.when(me + ways < n)
    def _():
        pl.semaphore_signal(barrier, inc=1, device_id={"ctx": me + ways}, device_id_type=MESH)

    @pl.when(me >= ways)
    def _():
        pl.semaphore_signal(barrier, inc=1, device_id={"ctx": me - ways}, device_id_type=MESH)

    pl.semaphore_wait(
        barrier, ways + (me + ways < n).astype(jnp.int32) + (me >= ways).astype(jnp.int32)
    )

    send(-1, 0)
    for head in range(kv_heads):
        send(-1, 1 + 2 * head)

    lane = lax.broadcasted_iota(jnp.int32, (1, HEAD), 1)
    step = lax.rem(lane, HEAD // 2).astype(jnp.float32)
    frequency = jnp.exp(step * (-2.0 * math.log(1000000.0) / HEAD))
    position = me * rows + lax.broadcasted_iota(jnp.int32, (rows, 1), 0)
    angles = position.astype(jnp.float32) * frequency
    cosine = jnp.cos(angles)
    sine = jnp.where(lane < HEAD // 2, -1.0, 1.0) * jnp.sin(angles)

    def rotated(entries):
        wide = entries.astype(jnp.float32)
        return (wide * cosine + pltpu.roll(wide, HEAD // 2, 1) * sine).astype(jnp.bfloat16)

    for head in range(kv_heads):
        k_own[head] = rotated(k_ref[:, head * HEAD : (head + 1) * HEAD])
        send(-1, 2 + 2 * head)
    load.wait()
    for head in range(q_heads):
        q_rot[head] = rotated(q_in[:, head * HEAD : (head + 1) * HEAD])

    valid = valid_ref[0]
    row_at = lax.broadcasted_iota(jnp.int32, (rows, rows), 0)
    col_at = lax.broadcasted_iota(jnp.int32, (rows, rows), 1)
    seg_row = seg_ref[...]
    seg_col = jnp.sum(jnp.where(row_at == col_at, seg_row, 0), axis=1, keepdims=True)
    ones = jnp.ones((2 * rows, HEAD), jnp.bfloat16)

    def scores_of(head, keys, bias):
        s = lax.dot_general(
            q_rot[head], keys, (((1,), (1,)), ((), ())), preferred_element_type=jnp.float32
        )
        return s * SCALE + bias

    causal = (seg_row == seg_col) & (col_at <= row_at)
    causal = causal & ((me * rows + col_at < valid) | (col_at == row_at))
    bias_ref[:, :rows] = jnp.where(causal, 0.0, BLOCKED)
    per_step = min(4, group)

    def first(head):
        kv = head // group
        t = scores_of(head, k_own[kv], bias_ref[:, :rows])
        top = jnp.max(t, axis=1, keepdims=True)
        p = jnp.exp2(t - top).astype(jnp.bfloat16)
        v = jnp.concatenate([v_ref[:, kv * HEAD : (kv + 1) * HEAD], ones[:rows]], axis=1)
        acc_ref[head] = jnp.dot(p, v, preferred_element_type=jnp.float32)
        max_ref[head] = jnp.broadcast_to(top, (rows, LANES))

    for head in range(q_heads):
        first(head)

    def later(stage, kv, last):
        span = pl.ds(2 * stage * rows, 2 * rows)

        def body(step, carry):
            for inner in range(per_step):
                head = kv * group + step * per_step + inner
                t = scores_of(head, k_buf[kv, span], bias_ref[...])
                before = max_ref[head]
                top = jnp.maximum(jnp.max(t, axis=1, keepdims=True), before[:, :1])
                p = jnp.exp2(t - top).astype(jnp.bfloat16)
                v = jnp.concatenate([v_buf[kv, span], ones], axis=1)
                mixed = jnp.dot(p, v, preferred_element_type=jnp.float32)
                total = acc_ref[head] * jnp.exp2(before[:, :1] - top) + mixed
                if last:
                    out = total[:, :HEAD] / total[:, HEAD:]
                    out = jnp.where(position < valid, out, 0.0)
                    rew_acc[...] += out * weight_ref[pl.ds(head, 1), :]
                    columns = pl.ds(pl.multiple_of(head * HEAD, HEAD), HEAD)
                    out_buf[:, columns] = out.astype(jnp.bfloat16)
                else:
                    acc_ref[head] = total
                    max_ref[head] = jnp.broadcast_to(top, (rows, LANES))
            return carry

        lax.fori_loop(0, group // per_step, body, 0)

    rew_acc[...] = jnp.zeros_like(rew_acc)
    stages = window // 2
    lane_at = lax.broadcasted_iota(jnp.int32, (1, 2 * rows), 1)
    second = (lane_at >= rows).astype(jnp.int32)
    stores = []
    for stage in range(stages):
        near, far = 2 * stage, 2 * stage + 1
        order = (far, near) if ways == 2 else (near, far)
        for slot in order:
            arrive(slot, 0)
        seg_keys = jnp.concatenate([seg_buf[near][:, :rows], seg_buf[far][:, :rows]], axis=1)
        key_pos = (me - 1 - near - second) * rows + lane_at - second * rows
        allowed = (seg_keys == seg_col) & (key_pos >= 0) & (key_pos < valid)
        bias_ref[...] = jnp.where(allowed, 0.0, BLOCKED)
        last = stage == stages - 1
        if not last:
            for slot in order:
                for chunk in range(1, chunks):
                    arrive(slot, chunk)
        for kv in range(kv_heads):
            if last:
                for slot in order:
                    arrive(slot, 1 + 2 * kv)
                    arrive(slot, 2 + 2 * kv)
                if ways == 2 and kv == 0 and kv_heads > 1:
                    pass
            later(stage, kv, last)
            if last:
                columns = pl.ds(kv * group * HEAD, group * HEAD)
                store = pltpu.make_async_copy(
                    out_buf.at[:, columns], out_hbm.at[:, columns], local_sem.at[1 + kv]
                )
                store.start()
                stores.append(store)

    mine = jnp.sum(rew_acc[...], axis=1, keepdims=True)
    mine_row = jnp.sum(jnp.where(row_at == col_at, mine, 0.0), axis=0, keepdims=True)
    rew_own[...] = jnp.zeros_like(rew_own)
    rew_own[:, :rows] = mine_row
    swap = pltpu.make_async_remote_copy(
        src_ref=rew_own,
        dst_ref=rew_far,
        send_sem=rew_sem.at[0],
        recv_sem=rew_sem.at[1],
        device_id={"tp": other},
        device_id_type=MESH,
    )
    swap.start()
    for slot in range(-1, window):
        for chunk in range(chunks):
            finish_send(slot, chunk)
    swap.wait()
    reward_ref[...] = mine_row + rew_far[:, :rows]
    for store in stores:
        store.wait()


def per_device(n, queries, keys, values, segments, valid_length, reward_weight):
    rows = queries.shape[0]
    q_heads = queries.shape[1] // HEAD
    kv_heads = keys.shape[1] // HEAD
    span = rows * n // 2
    window = -(-(span - 1) // rows)
    window += window % 2
    ways = 2 if n <= 8 else 1
    chunks = 1 + 2 * kv_heads
    wide = -(-rows // LANES) * LANES
    vmem = pl.BlockSpec(memory_space=pltpu.VMEM)
    attention, reward = pl.pallas_call(
        functools.partial(kernel, n, window, ways),
        out_shape=(
            jax.ShapeDtypeStruct(queries.shape, jnp.bfloat16),
            jax.ShapeDtypeStruct((1, rows), jnp.float32),
        ),
        in_specs=[
            pl.BlockSpec(memory_space=pl.ANY),
            vmem,
            vmem,
            vmem,
            pl.BlockSpec(memory_space=pltpu.SMEM),
            vmem,
        ],
        out_specs=(pl.BlockSpec(memory_space=pl.ANY), vmem),
        scratch_shapes=[
            pltpu.VMEM(queries.shape, jnp.bfloat16),
            pltpu.VMEM((q_heads, rows, HEAD), jnp.bfloat16),
            pltpu.VMEM((kv_heads, rows, HEAD), jnp.bfloat16),
            pltpu.VMEM((kv_heads, window * rows, HEAD), jnp.bfloat16),
            pltpu.VMEM((kv_heads, window * rows, HEAD), jnp.bfloat16),
            pltpu.VMEM((1, wide), jnp.int32),
            pltpu.VMEM((window, 1, wide), jnp.int32),
            pltpu.VMEM((rows, 2 * rows), jnp.float32),
            pltpu.VMEM((q_heads, rows, LANES), jnp.float32),
            pltpu.VMEM((q_heads, rows, 2 * HEAD), jnp.float32),
            pltpu.VMEM(queries.shape, jnp.bfloat16),
            pltpu.VMEM((rows, HEAD), jnp.float32),
            pltpu.VMEM((1, wide), jnp.float32),
            pltpu.VMEM((1, wide), jnp.float32),
            pltpu.SemaphoreType.DMA((3, window, chunks)),
            pltpu.SemaphoreType.DMA((window, chunks)),
            pltpu.SemaphoreType.DMA((1 + kv_heads,)),
            pltpu.SemaphoreType.DMA((2,)),
        ],
        compiler_params=pltpu.CompilerParams(
            collective_id=0, has_side_effects=True, vmem_limit_bytes=48 * 1024 * 1024
        ),
    )(
        queries,
        keys,
        values,
        segments.reshape(1, rows),
        valid_length,
        reward_weight.reshape(q_heads, HEAD),
    )
    return attention, reward.reshape(rows)


def solution(mesh):
    return jax.shard_map(
        functools.partial(per_device, mesh.shape["ctx"]),
        mesh=mesh,
        in_specs=(
            P(("groups", "ctx"), "tp"),
            P(("groups", "ctx"), "tp"),
            P(("groups", "ctx"), "tp"),
            P(("groups", "ctx")),
            P("groups"),
            P("tp"),
        ),
        out_specs=(P(("groups", "ctx"), "tp"), P(("groups", "ctx"))),
        check_vma=False,
    )
```

```python
import functools
import math

import jax
import jax.numpy as jnp
from jax import lax
from jax.experimental import pallas as pl
from jax.experimental.pallas import tpu as pltpu
from jax.sharding import PartitionSpec as P

HEAD = 128
LANES = 128
MESH = pl.DeviceIdType.MESH
SCALE = HEAD**-0.5 * math.log2(math.e)
BLOCKED = -1e30


def kernel(
    n,
    window,
    ways,
    q_hbm,
    k_hbm,
    v_hbm,
    seg_hbm,
    valid_ref,
    weight_hbm,
    out_hbm,
    reward_ref,
    q_in,
    k_ref,
    v_ref,
    seg_ref,
    weight_ref,
    q_rot,
    k_own,
    k_buf,
    v_buf,
    seg_own,
    seg_buf,
    bias_ref,
    max_ref,
    acc_ref,
    out_buf,
    rew_acc,
    rew_own,
    rew_far,
    send_sem,
    recv_sem,
    local_sem,
    rew_sem,
    load_sem,
):
    rows = k_ref.shape[0]
    kv_heads = k_ref.shape[1] // HEAD
    q_heads = q_in.shape[1] // HEAD
    group = q_heads // kv_heads
    chunks = 1 + 2 * kv_heads
    me = lax.axis_index("ctx")
    other = 1 - lax.axis_index("tp")
    odd = lax.rem(me, 2)

    barrier = pltpu.get_barrier_semaphore()
    pl.semaphore_signal(barrier, inc=1, device_id={"tp": other}, device_id_type=MESH)
    if ways == 2:
        pl.semaphore_signal(barrier, inc=1, device_id={"ctx": me + 1 - 2 * odd}, device_id_type=MESH)

    @pl.when(me + ways < n)
    def _():
        pl.semaphore_signal(barrier, inc=1, device_id={"ctx": me + ways}, device_id_type=MESH)

    @pl.when(me >= ways)
    def _():
        pl.semaphore_signal(barrier, inc=1, device_id={"ctx": me - ways}, device_id_type=MESH)

    loads = []
    pairs = ((v_hbm, v_ref), (seg_hbm, seg_ref), (k_hbm, k_ref), (q_hbm, q_in), (weight_hbm, weight_ref))
    for at, (source, target) in enumerate(pairs):
        loads.append(pltpu.make_async_copy(source, target, load_sem.at[at]))
        loads[-1].start()

    def outgoing(slot):
        held = me - 1 - slot >= 0
        if ways == 1:
            return [(0, slot + 1, me + 1, held & (me + 1 < n))] if slot + 1 < window else []
        sends = []
        if slot == -1 or slot % 2 == 1:
            if slot + 2 < window:
                sends.append((0, slot + 2, me + 2, held & (me + 2 < n)))
            if slot + 1 < window:
                sends.append((1, slot + 1, me + 1, held & (odd == 0)))
            if slot >= 1:
                sends.append((2, slot - 1, me - 1, held & (odd == 1)))
        return sends

    def piece(slot, chunk):
        if chunk == 0:
            return seg_own if slot < 0 else seg_buf.at[slot]
        head, is_key = (chunk - 1) // 2, (chunk - 1) % 2 == 1
        if slot < 0:
            return k_own.at[head] if is_key else v_ref.at[:, pl.ds(head * HEAD, HEAD)]
        return (k_buf if is_key else v_buf).at[head, pl.ds(slot * rows, rows)]

    def copy_of(slot, chunk, path, there, device):
        return pltpu.make_async_remote_copy(
            src_ref=piece(slot, chunk),
            dst_ref=piece(there, chunk),
            send_sem=send_sem.at[path, there, chunk],
            recv_sem=recv_sem.at[there, chunk],
            device_id={"ctx": device},
            device_id_type=MESH,
        )

    def send(slot, chunk):
        for path, there, device, condition in outgoing(slot):
            @pl.when(condition)
            def _(path=path, there=there, device=device):
                copy_of(slot, chunk, path, there, device).start()

    def finish_send(slot, chunk):
        for path, there, device, condition in outgoing(slot):
            @pl.when(condition)
            def _(path=path, there=there, device=device):
                copy_of(slot, chunk, path, there, device).wait_send()

    def arrive(slot, chunk):
        @pl.when(me - 1 - slot >= 0)
        def _():
            copy_of(slot, chunk, 0, slot, me).wait_recv()

        send(slot, chunk)

    for slot in range(window):
        @pl.when(me - 1 - slot < 0)
        def _(slot=slot):
            seg_buf[slot] = jnp.zeros(seg_buf.shape[1:], seg_buf.dtype)
            for head in range(kv_heads):
                k_buf[head, slot * rows : (slot + 1) * rows] = jnp.zeros((rows, HEAD), k_buf.dtype)
                v_buf[head, slot * rows : (slot + 1) * rows] = jnp.zeros((rows, HEAD), v_buf.dtype)

    loads[1].wait()
    seg_own[...] = jnp.zeros_like(seg_own)
    seg_own[:, :rows] = seg_ref[...]
    loads[0].wait()
    pl.semaphore_wait(
        barrier, ways + (me + ways < n).astype(jnp.int32) + (me >= ways).astype(jnp.int32)
    )

    send(-1, 0)
    for head in range(kv_heads):
        send(-1, 1 + 2 * head)

    lane = lax.broadcasted_iota(jnp.int32, (1, HEAD), 1)
    step = lax.rem(lane, HEAD // 2).astype(jnp.float32)
    frequency = jnp.exp(step * (-2.0 * math.log(1000000.0) / HEAD))
    position = me * rows + lax.broadcasted_iota(jnp.int32, (rows, 1), 0)
    angles = position.astype(jnp.float32) * frequency
    cosine = jnp.cos(angles)
    sine = jnp.where(lane < HEAD // 2, -1.0, 1.0) * jnp.sin(angles)

    def rotated(entries):
        wide = entries.astype(jnp.float32)
        return (wide * cosine + pltpu.roll(wide, HEAD // 2, 1) * sine).astype(jnp.bfloat16)

    loads[2].wait()
    for head in range(kv_heads):
        k_own[head] = rotated(k_ref[:, head * HEAD : (head + 1) * HEAD])
        send(-1, 2 + 2 * head)
    loads[3].wait()
    for head in range(q_heads):
        q_rot[head] = rotated(q_in[:, head * HEAD : (head + 1) * HEAD])

    valid = valid_ref[0]
    row_at = lax.broadcasted_iota(jnp.int32, (rows, rows), 0)
    col_at = lax.broadcasted_iota(jnp.int32, (rows, rows), 1)
    seg_row = seg_ref[...]
    seg_col = jnp.sum(jnp.where(row_at == col_at, seg_row, 0), axis=1, keepdims=True)
    ones = jnp.ones((2 * rows, HEAD), jnp.bfloat16)

    def scores_of(head, keys, bias):
        s = lax.dot_general(
            q_rot[head], keys, (((1,), (1,)), ((), ())), preferred_element_type=jnp.float32
        )
        return s * SCALE + bias

    causal = (seg_row == seg_col) & (col_at <= row_at)
    causal = causal & ((me * rows + col_at < valid) | (col_at == row_at))
    bias_ref[:, :rows] = jnp.where(causal, 0.0, BLOCKED)
    per_step = min(4, group)

    def first(head):
        kv = head // group
        t = scores_of(head, k_own[kv], bias_ref[:, :rows])
        top = jnp.max(t, axis=1, keepdims=True)
        p = jnp.exp2(t - top).astype(jnp.bfloat16)
        v = jnp.concatenate([v_ref[:, kv * HEAD : (kv + 1) * HEAD], ones[:rows]], axis=1)
        acc_ref[head] = jnp.dot(p, v, preferred_element_type=jnp.float32)
        max_ref[head] = jnp.broadcast_to(top, (rows, LANES))

    for head in range(q_heads):
        first(head)

    def later(stage, kv, last):
        span = pl.ds(2 * stage * rows, 2 * rows)

        def body(step, carry):
            for inner in range(per_step):
                head = kv * group + step * per_step + inner
                t = scores_of(head, k_buf[kv, span], bias_ref[...])
                before = max_ref[head]
                top = jnp.maximum(jnp.max(t, axis=1, keepdims=True), before[:, :1])
                p = jnp.exp2(t - top).astype(jnp.bfloat16)
                v = jnp.concatenate([v_buf[kv, span], ones], axis=1)
                mixed = jnp.dot(p, v, preferred_element_type=jnp.float32)
                total = acc_ref[head] * jnp.exp2(before[:, :1] - top) + mixed
                if last:
                    out = total[:, :HEAD] / total[:, HEAD:]
                    out = jnp.where(position < valid, out, 0.0)
                    rew_acc[...] += out * weight_ref[pl.ds(head, 1), :]
                    columns = pl.ds(pl.multiple_of(head * HEAD, HEAD), HEAD)
                    out_buf[:, columns] = out.astype(jnp.bfloat16)
                else:
                    acc_ref[head] = total
                    max_ref[head] = jnp.broadcast_to(top, (rows, LANES))
            return carry

        lax.fori_loop(0, group // per_step, body, 0)

    loads[4].wait()
    rew_acc[...] = jnp.zeros_like(rew_acc)
    stages = window // 2
    lane_at = lax.broadcasted_iota(jnp.int32, (1, 2 * rows), 1)
    second = (lane_at >= rows).astype(jnp.int32)
    stores = []
    for stage in range(stages):
        near, far = 2 * stage, 2 * stage + 1
        order = (far, near) if ways == 2 else (near, far)
        for slot in order:
            arrive(slot, 0)
        seg_keys = jnp.concatenate([seg_buf[near][:, :rows], seg_buf[far][:, :rows]], axis=1)
        key_pos = (me - 1 - near - second) * rows + lane_at - second * rows
        allowed = (seg_keys == seg_col) & (key_pos >= 0) & (key_pos < valid)
        bias_ref[...] = jnp.where(allowed, 0.0, BLOCKED)
        last = stage == stages - 1
        if not last:
            for slot in order:
                for chunk in range(1, chunks):
                    arrive(slot, chunk)
        for kv in range(kv_heads):
            if last:
                for slot in order:
                    arrive(slot, 1 + 2 * kv)
                    arrive(slot, 2 + 2 * kv)
            later(stage, kv, last)
            if last:
                columns = pl.ds(kv * group * HEAD, group * HEAD)
                store = pltpu.make_async_copy(
                    out_buf.at[:, columns], out_hbm.at[:, columns], local_sem.at[1 + kv]
                )
                store.start()
                stores.append(store)

    mine = jnp.sum(rew_acc[...], axis=1, keepdims=True)
    mine_row = jnp.sum(jnp.where(row_at == col_at, mine, 0.0), axis=0, keepdims=True)
    rew_own[...] = jnp.zeros_like(rew_own)
    rew_own[:, :rows] = mine_row
    swap = pltpu.make_async_remote_copy(
        src_ref=rew_own,
        dst_ref=rew_far,
        send_sem=rew_sem.at[0],
        recv_sem=rew_sem.at[1],
        device_id={"tp": other},
        device_id_type=MESH,
    )
    swap.start()
    for slot in range(-1, window):
        for chunk in range(chunks):
            finish_send(slot, chunk)
    swap.wait()
    reward_ref[...] = mine_row + rew_far[:, :rows]
    for store in stores:
        store.wait()


def per_device(n, queries, keys, values, segments, valid_length, reward_weight):
    rows = queries.shape[0]
    q_heads = queries.shape[1] // HEAD
    kv_heads = keys.shape[1] // HEAD
    span = rows * n // 2
    window = -(-(span - 1) // rows)
    window += window % 2
    ways = 2 if n <= 8 else 1
    chunks = 1 + 2 * kv_heads
    wide = -(-rows // LANES) * LANES
    vmem = pl.BlockSpec(memory_space=pltpu.VMEM)
    hbm = pl.BlockSpec(memory_space=pl.ANY)
    attention, reward = pl.pallas_call(
        functools.partial(kernel, n, window, ways),
        out_shape=(
            jax.ShapeDtypeStruct(queries.shape, jnp.bfloat16),
            jax.ShapeDtypeStruct((1, rows), jnp.float32),
        ),
        in_specs=[
            hbm,
            hbm,
            hbm,
            hbm,
            pl.BlockSpec(memory_space=pltpu.SMEM),
            hbm,
        ],
        out_specs=(hbm, vmem),
        scratch_shapes=[
            pltpu.VMEM(queries.shape, jnp.bfloat16),
            pltpu.VMEM(keys.shape, jnp.bfloat16),
            pltpu.VMEM(values.shape, jnp.bfloat16),
            pltpu.VMEM((1, rows), jnp.int32),
            pltpu.VMEM((q_heads, HEAD), jnp.float32),
            pltpu.VMEM((q_heads, rows, HEAD), jnp.bfloat16),
            pltpu.VMEM((kv_heads, rows, HEAD), jnp.bfloat16),
            pltpu.VMEM((kv_heads, window * rows, HEAD), jnp.bfloat16),
            pltpu.VMEM((kv_heads, window * rows, HEAD), jnp.bfloat16),
            pltpu.VMEM((1, wide), jnp.int32),
            pltpu.VMEM((window, 1, wide), jnp.int32),
            pltpu.VMEM((rows, 2 * rows), jnp.float32),
            pltpu.VMEM((q_heads, rows, LANES), jnp.float32),
            pltpu.VMEM((q_heads, rows, 2 * HEAD), jnp.float32),
            pltpu.VMEM(queries.shape, jnp.bfloat16),
            pltpu.VMEM((rows, HEAD), jnp.float32),
            pltpu.VMEM((1, wide), jnp.float32),
            pltpu.VMEM((1, wide), jnp.float32),
            pltpu.SemaphoreType.DMA((3, window, chunks)),
            pltpu.SemaphoreType.DMA((window, chunks)),
            pltpu.SemaphoreType.DMA((1 + kv_heads,)),
            pltpu.SemaphoreType.DMA((2,)),
            pltpu.SemaphoreType.DMA((5,)),
        ],
        compiler_params=pltpu.CompilerParams(
            collective_id=0, has_side_effects=True, vmem_limit_bytes=60 * 1024 * 1024
        ),
    )(
        queries,
        keys,
        values,
        segments.reshape(1, rows),
        valid_length,
        reward_weight.reshape(q_heads, HEAD),
    )
    return attention, reward.reshape(rows)


def solution(mesh):
    return jax.shard_map(
        functools.partial(per_device, mesh.shape["ctx"]),
        mesh=mesh,
        in_specs=(
            P(("groups", "ctx"), "tp"),
            P(("groups", "ctx"), "tp"),
            P(("groups", "ctx"), "tp"),
            P(("groups", "ctx")),
            P("groups"),
            P("tp"),
        ),
        out_specs=(P(("groups", "ctx"), "tp"), P(("groups", "ctx"))),
        check_vma=False,
    )
```

```python
import functools
import math

import jax
import jax.numpy as jnp
from jax import lax
from jax.experimental import pallas as pl
from jax.experimental.pallas import tpu as pltpu
from jax.sharding import PartitionSpec as P

HEAD = 128
LANES = 128
MESH = pl.DeviceIdType.MESH
SCALE = HEAD**-0.5 * math.log2(math.e)
BLOCKED = -1e30
BATCH = 4
PART = 96


def kernel(
    n,
    window,
    ways,
    q_hbm,
    k_hbm,
    v_hbm,
    seg_hbm,
    valid_hbm,
    weight_hbm,
    out_buf,
    reward_ref,
    q_in,
    k_ref,
    v_ref,
    seg_ref,
    weight_ref,
    valid_ref,
    q_rot,
    k_own,
    k_buf,
    v_buf,
    seg_own,
    seg_buf,
    bias_ref,
    max_ref,
    acc_ref,
    rew_acc,
    rew_own,
    rew_far,
    send_sem,
    recv_sem,
    rew_sem,
    load_sem,
):
    rows = k_ref.shape[0]
    kv_heads = k_ref.shape[1] // HEAD
    q_heads = q_in.shape[1] // HEAD
    group = q_heads // kv_heads
    chunks = 1 + 2 * kv_heads
    me = lax.axis_index("ctx")
    other = 1 - lax.axis_index("tp")
    odd = lax.rem(me, 2)

    barrier = pltpu.get_barrier_semaphore()
    pl.semaphore_signal(barrier, inc=1, device_id={"tp": other}, device_id_type=MESH)
    if ways == 2:
        pl.semaphore_signal(barrier, inc=1, device_id={"ctx": me + 1 - 2 * odd}, device_id_type=MESH)

    @pl.when(me + ways < n)
    def _():
        pl.semaphore_signal(barrier, inc=1, device_id={"ctx": me + ways}, device_id_type=MESH)

    @pl.when(me >= ways)
    def _():
        pl.semaphore_signal(barrier, inc=1, device_id={"ctx": me - ways}, device_id_type=MESH)

    loads = []
    pairs = ((v_hbm, v_ref), (seg_hbm, seg_ref), (k_hbm, k_ref), (q_hbm, q_in), (weight_hbm, weight_ref), (valid_hbm, valid_ref))
    for at, (source, target) in enumerate(pairs):
        loads.append(pltpu.make_async_copy(source, target, load_sem.at[at]))
        loads[-1].start()

    def outgoing(slot):
        held = me - 1 - slot >= 0
        if ways == 1:
            return [(0, slot + 1, me + 1, held & (me + 1 < n))] if slot + 1 < window else []
        sends = []
        if slot == -1 or slot % 2 == 1:
            if slot + 2 < window:
                sends.append((0, slot + 2, me + 2, held & (me + 2 < n)))
            if slot + 1 < window:
                sends.append((1, slot + 1, me + 1, held & (odd == 0)))
            if slot >= 1:
                sends.append((2, slot - 1, me - 1, held & (odd == 1)))
        return sends

    def piece(slot, chunk):
        if chunk == 0:
            return seg_own if slot < 0 else seg_buf.at[slot]
        head, is_key = (chunk - 1) // 2, (chunk - 1) % 2 == 1
        if slot < 0:
            return k_own.at[head] if is_key else v_ref.at[:, pl.ds(head * HEAD, HEAD)]
        return (k_buf if is_key else v_buf).at[head, pl.ds(slot * rows, rows)]

    def copy_of(slot, chunk, path, there, device):
        return pltpu.make_async_remote_copy(
            src_ref=piece(slot, chunk),
            dst_ref=piece(there, chunk),
            send_sem=send_sem.at[path, there, chunk],
            recv_sem=recv_sem.at[there, chunk],
            device_id={"ctx": device},
            device_id_type=MESH,
        )

    def send(slot, chunk):
        for path, there, device, condition in outgoing(slot):
            @pl.when(condition)
            def _(path=path, there=there, device=device):
                copy_of(slot, chunk, path, there, device).start()

    def finish_send(slot, chunk):
        for path, there, device, condition in outgoing(slot):
            @pl.when(condition)
            def _(path=path, there=there, device=device):
                copy_of(slot, chunk, path, there, device).wait_send()

    arrived = set()

    def arrive(slot, chunk):
        if slot >= window or chunk >= chunks or (slot, chunk) in arrived:
            return
        arrived.add((slot, chunk))

        @pl.when(me - 1 - slot >= 0)
        def _():
            copy_of(slot, chunk, 0, slot, me).wait_recv()

        send(slot, chunk)

    for slot in range(window):
        @pl.when(me - 1 - slot < 0)
        def _(slot=slot):
            seg_buf[slot] = jnp.zeros(seg_buf.shape[1:], seg_buf.dtype)
            for head in range(kv_heads):
                k_buf[head, slot * rows : (slot + 1) * rows] = jnp.zeros((rows, HEAD), k_buf.dtype)
                v_buf[head, slot * rows : (slot + 1) * rows] = jnp.zeros((rows, HEAD), v_buf.dtype)

    loads[1].wait()
    seg_own[...] = jnp.zeros_like(seg_own)
    seg_own[:, :rows] = seg_ref[...]
    lane = lax.broadcasted_iota(jnp.int32, (1, HEAD), 1)
    step = lax.rem(lane, HEAD // 2).astype(jnp.float32)
    frequency = jnp.exp(step * (-2.0 * math.log(1000000.0) / HEAD))
    position = me * rows + lax.broadcasted_iota(jnp.int32, (rows, 1), 0)
    angles = position.astype(jnp.float32) * frequency
    cosine = jnp.cos(angles)
    sine = jnp.where(lane < HEAD // 2, -1.0, 1.0) * jnp.sin(angles)

    def rotated(entries):
        wide = entries.astype(jnp.float32)
        return (wide * cosine + pltpu.roll(wide, HEAD // 2, 1) * sine).astype(jnp.bfloat16)

    loads[2].wait()
    for head in range(kv_heads):
        k_own[head] = rotated(k_ref[:, head * HEAD : (head + 1) * HEAD])
    loads[0].wait()

    pl.semaphore_wait(
        barrier, ways + (me + ways < n).astype(jnp.int32) + (me >= ways).astype(jnp.int32)
    )

    for chunk in range(chunks):
        send(-1, chunk)

    loads[3].wait()
    for head in range(q_heads):
        q_rot[head] = rotated(q_in[:, head * HEAD : (head + 1) * HEAD])

    loads[5].wait()
    valid = valid_ref[0]
    row_at = lax.broadcasted_iota(jnp.int32, (rows, rows), 0)
    col_at = lax.broadcasted_iota(jnp.int32, (rows, rows), 1)
    seg_row = seg_ref[...]
    seg_col = jnp.sum(jnp.where(row_at == col_at, seg_row, 0), axis=1, keepdims=True)
    ones = jnp.ones((2 * rows, HEAD), jnp.bfloat16)

    def attend(head0, count, keys, values, bias, before, total):
        width = keys.shape[0]
        tiles = -(-width // LANES)
        held = jnp.concatenate([values, ones[:width]], axis=1)
        results = []
        for part in range(0, count, BATCH):
            q = q_rot[pl.ds(head0 + part, BATCH)].reshape(BATCH * rows, HEAD)
            s = lax.dot_general(
                q, keys, (((1,), (1,)), ((), ())), preferred_element_type=jnp.float32
            )
            for i in range(BATCH):
                for r in range(0, rows, PART):
                    t = s[i * rows + r : i * rows + r + PART] * SCALE + bias[r : r + PART]
                    top = jnp.broadcast_to(jnp.max(t, axis=1, keepdims=True), (PART, LANES))
                    if before is not None:
                        old = before[head0 + part + i, r : r + PART]
                        top = jnp.maximum(top, old)
                    wide = jnp.concatenate([top] * tiles, axis=1)[:, :width]
                    p = jnp.exp2(t - wide).astype(jnp.bfloat16)
                    mixed = jnp.dot(p, held, preferred_element_type=jnp.float32)
                    if before is not None:
                        alpha = jnp.exp2(old - top)
                        mixed += total[head0 + part + i, r : r + PART] * jnp.concatenate([alpha, alpha], axis=1)
                    results.append((part + i, r, top, mixed))
        return results

    causal = (seg_row == seg_col) & (col_at <= row_at)
    causal = causal & ((me * rows + col_at < valid) | (col_at == row_at))
    bias_ref[:, :rows] = jnp.where(causal, 0.0, BLOCKED)
    per_step = min(4, group)

    def keep(head0, results):
        for i, r, top, mixed in results:
            acc_ref[head0 + i, r : r + PART] = mixed
            max_ref[head0 + i, r : r + PART] = top

    lead = ways - 1
    polls = [(0,), (1,), (2,), ()]
    for kv in range(kv_heads):
        for step in range(group // per_step):
            here = kv * group + step * per_step
            values = v_ref[:, kv * HEAD : (kv + 1) * HEAD]
            keep(here, attend(here, per_step, k_own[kv], values, bias_ref[:, :rows], None, None))
            for chunk in polls.pop(0) if polls else ():
                arrive(lead, chunk)

    def later(stage, kv, step, last):
        span = pl.ds(2 * stage * rows, 2 * rows)
        head0 = kv * group + step * per_step
        results = attend(head0, per_step, k_buf[kv, span], v_buf[kv, span], bias_ref[...], max_ref, acc_ref)
        if not last:
            keep(head0, results)
            return
        for i, r, top, mixed in results:
            out = mixed[:, :HEAD] / mixed[:, HEAD:]
            out = jnp.where(position[r : r + PART] < valid, out, 0.0)
            rew_acc[r : r + PART] += out * weight_ref[pl.ds(head0 + i, 1), :]
            out_buf[r : r + PART, pl.ds((head0 + i) * HEAD, HEAD)] = out.astype(jnp.bfloat16)

    loads[4].wait()
    rew_acc[...] = jnp.zeros_like(rew_acc)
    stages = window // 2
    lane_at = lax.broadcasted_iota(jnp.int32, (1, 2 * rows), 1)
    second = (lane_at >= rows).astype(jnp.int32)
    for stage in range(stages):
        near, far = 2 * stage, 2 * stage + 1
        order = (far, near) if ways == 2 else (near, far)
        for slot in order:
            arrive(slot, 0)
        seg_keys = jnp.concatenate([seg_buf[near][:, :rows], seg_buf[far][:, :rows]], axis=1)
        key_pos = (me - 1 - near - second) * rows + lane_at - second * rows
        allowed = (seg_keys == seg_col) & (key_pos >= 0) & (key_pos < valid)
        bias_ref[...] = jnp.where(allowed, 0.0, BLOCKED)
        last = stage == stages - 1
        for kv in range(kv_heads):
            for slot in order:
                arrive(slot, 1 + 2 * kv)
                arrive(slot, 2 + 2 * kv)
            steps = group // per_step
            for step in range(steps):
                later(stage, kv, step, last)
                ahead = 2 * stage + lead + (0 if kv + 1 < kv_heads else 2)
                after = 1 + 2 * (kv + 1) if kv + 1 < kv_heads else 1
                if ahead > 2 * stage + 1:
                    arrive(ahead, 0)
                if step < 2:
                    arrive(ahead, after + step)

    mine = jnp.sum(rew_acc[...], axis=1, keepdims=True)
    mine_row = jnp.sum(jnp.where(row_at == col_at, mine, 0.0), axis=0, keepdims=True)
    rew_own[...] = jnp.zeros_like(rew_own)
    rew_own[:, :rows] = mine_row
    swap = pltpu.make_async_remote_copy(
        src_ref=rew_own,
        dst_ref=rew_far,
        send_sem=rew_sem.at[0],
        recv_sem=rew_sem.at[1],
        device_id={"tp": other},
        device_id_type=MESH,
    )
    swap.start()
    for slot in range(-1, window):
        for chunk in range(chunks):
            finish_send(slot, chunk)
    swap.wait()
    reward_ref[...] = mine_row + rew_far[:, :rows]


def per_device(n, queries, keys, values, segments, valid_length, reward_weight):
    rows = queries.shape[0]
    q_heads = queries.shape[1] // HEAD
    kv_heads = keys.shape[1] // HEAD
    span = rows * n // 2
    window = -(-(span - 1) // rows)
    window += window % 2
    ways = 2 if n <= 8 else 1
    chunks = 1 + 2 * kv_heads
    wide = -(-rows // LANES) * LANES
    vmem = pl.BlockSpec(memory_space=pltpu.VMEM)
    hbm = pl.BlockSpec(memory_space=pltpu.HBM)
    attention, reward = pl.pallas_call(
        functools.partial(kernel, n, window, ways),
        out_shape=(
            jax.ShapeDtypeStruct(queries.shape, jnp.bfloat16),
            jax.ShapeDtypeStruct((1, rows), jnp.float32),
        ),
        in_specs=[
            hbm,
            hbm,
            hbm,
            hbm,
            hbm,
            hbm,
        ],
        out_specs=(vmem, vmem),
        scratch_shapes=[
            pltpu.VMEM(queries.shape, jnp.bfloat16),
            pltpu.VMEM(keys.shape, jnp.bfloat16),
            pltpu.VMEM(values.shape, jnp.bfloat16),
            pltpu.VMEM((1, rows), jnp.int32),
            pltpu.VMEM((q_heads, HEAD), jnp.float32),
            pltpu.SMEM((1,), jnp.int32),
            pltpu.VMEM((q_heads, rows, HEAD), jnp.bfloat16),
            pltpu.VMEM((kv_heads, rows, HEAD), jnp.bfloat16),
            pltpu.VMEM((kv_heads, window * rows, HEAD), jnp.bfloat16),
            pltpu.VMEM((kv_heads, window * rows, HEAD), jnp.bfloat16),
            pltpu.VMEM((1, wide), jnp.int32),
            pltpu.VMEM((window, 1, wide), jnp.int32),
            pltpu.VMEM((rows, 2 * rows), jnp.float32),
            pltpu.VMEM((q_heads, rows, LANES), jnp.float32),
            pltpu.VMEM((q_heads, rows, 2 * HEAD), jnp.float32),
            pltpu.VMEM((rows, HEAD), jnp.float32),
            pltpu.VMEM((1, wide), jnp.float32),
            pltpu.VMEM((1, wide), jnp.float32),
            pltpu.SemaphoreType.DMA((3, window, chunks)),
            pltpu.SemaphoreType.DMA((window, chunks)),
            pltpu.SemaphoreType.DMA((2,)),
            pltpu.SemaphoreType.DMA((6,)),
        ],
        compiler_params=pltpu.CompilerParams(
            collective_id=0, has_side_effects=True, vmem_limit_bytes=60 * 1024 * 1024
        ),
    )(
        queries,
        keys,
        values,
        segments.reshape(1, rows),
        valid_length,
        reward_weight.reshape(q_heads, HEAD),
    )
    return attention, reward.reshape(rows)


def solution(mesh):
    return jax.shard_map(
        functools.partial(per_device, mesh.shape["ctx"]),
        mesh=mesh,
        in_specs=(
            P(("groups", "ctx"), "tp"),
            P(("groups", "ctx"), "tp"),
            P(("groups", "ctx"), "tp"),
            P(("groups", "ctx")),
            P("groups"),
            P("tp"),
        ),
        out_specs=(P(("groups", "ctx"), "tp"), P(("groups", "ctx"))),
        check_vma=False,
    )
```

```python
import functools
import math

import jax
import jax.numpy as jnp
from jax import lax
from jax.experimental import pallas as pl
from jax.experimental.pallas import tpu as pltpu
from jax.sharding import PartitionSpec as P

HEAD = 128
LANES = 128
MESH = pl.DeviceIdType.MESH
SCALE = HEAD**-0.5 * math.log2(math.e)
BLOCKED = -1e30
BATCH = 4
PART = 96
PIECES = 1
COPIES = 4


def kernel(
    n,
    window,
    ways,
    q_hbm,
    k_hbm,
    v_hbm,
    seg_hbm,
    valid_hbm,
    weight_hbm,
    out_hbm,
    reward_ref,
    q_in,
    k_ref,
    v_ref,
    seg_ref,
    weight_ref,
    valid_ref,
    q_rot,
    k_own,
    k_buf,
    v_buf,
    seg_own,
    seg_buf,
    bias_ref,
    max_ref,
    acc_ref,
    out_buf,
    rew_acc,
    rew_own,
    rew_far,
    send_sem,
    recv_sem,
    rew_sem,
    load_sem,
    store_sem,
):
    rows = k_ref.shape[0]
    kv_heads = k_ref.shape[1] // HEAD
    q_heads = q_in.shape[1] // HEAD
    group = q_heads // kv_heads
    chunks = 1 + 2 * kv_heads * PIECES
    me = lax.axis_index("ctx")
    other = 1 - lax.axis_index("tp")
    odd = lax.rem(me, 2)

    barrier = pltpu.get_barrier_semaphore()
    pl.semaphore_signal(barrier, inc=1, device_id={"tp": other}, device_id_type=MESH)
    if ways == 2:
        pl.semaphore_signal(barrier, inc=1, device_id={"ctx": me + 1 - 2 * odd}, device_id_type=MESH)

    @pl.when(me + ways < n)
    def _():
        pl.semaphore_signal(barrier, inc=1, device_id={"ctx": me + ways}, device_id_type=MESH)

    @pl.when(me >= ways)
    def _():
        pl.semaphore_signal(barrier, inc=1, device_id={"ctx": me - ways}, device_id_type=MESH)

    loads = []
    pairs = ((v_hbm, v_ref), (seg_hbm, seg_ref), (k_hbm, k_ref), (q_hbm, q_in), (weight_hbm, weight_ref), (valid_hbm, valid_ref))
    for at, (source, target) in enumerate(pairs):
        loads.append(pltpu.make_async_copy(source, target, load_sem.at[at]))
        loads[-1].start()

    def outgoing(slot, chunk):
        held = me - 1 - slot >= 0
        if ways == 1:
            return [(0, slot + 1, me + 1, held & (me + 1 < n))] if slot + 1 < window else []
        sends = []
        late = chunk == chunks - 1
        if slot == -1 or slot % 2 == 1:
            if slot + 2 < window:
                sends.append((0, slot + 2, me + 2, held & (me + 2 < n)))
            if slot + 1 < window:
                sends.append((1, slot + 1, me + 1, held & (odd == 0)))
            if slot == 1 or (slot > 1 and not late):
                sends.append((2, slot - 1, me - 1, held & (odd == 1)))
        elif late and slot + 2 < window:
            sends.append((2, slot + 2, me + 2, held & (odd == 0) & (me + 2 < n)))
        return sends

    def piece(slot, chunk):
        if chunk == 0:
            return seg_own if slot < 0 else seg_buf.at[slot]
        which, part = (chunk - 1) // PIECES, (chunk - 1) % PIECES
        head, is_key = which // 2, which % 2 == 1
        size = rows // PIECES
        if slot < 0:
            own = pl.ds(part * size, size)
            return k_own.at[head, own] if is_key else v_ref.at[own, pl.ds(head * HEAD, HEAD)]
        return (k_buf if is_key else v_buf).at[head, pl.ds(slot * rows + part * size, size)]

    def copy_of(slot, chunk, path, there, device):
        return pltpu.make_async_remote_copy(
            src_ref=piece(slot, chunk),
            dst_ref=piece(there, chunk),
            send_sem=send_sem.at[path, there, chunk],
            recv_sem=recv_sem.at[there, chunk],
            device_id={"ctx": device},
            device_id_type=MESH,
        )

    def send(slot, chunk):
        for path, there, device, condition in outgoing(slot, chunk):
            @pl.when(condition)
            def _(path=path, there=there, device=device):
                copy_of(slot, chunk, path, there, device).start()

    def finish_send(slot, chunk):
        for path, there, device, condition in outgoing(slot, chunk):
            @pl.when(condition)
            def _(path=path, there=there, device=device):
                copy_of(slot, chunk, path, there, device).wait_send()

    arrived = set()

    def arrive(slot, which):
        if slot >= window or which > 2 * kv_heads or (slot, which) in arrived:
            return
        arrived.add((slot, which))
        for chunk in (0,) if which == 0 else range(1 + (which - 1) * PIECES, 1 + which * PIECES):
            @pl.when(me - 1 - slot >= 0)
            def _(chunk=chunk):
                copy_of(slot, chunk, 0, slot, me).wait_recv()

            send(slot, chunk)

    for slot in range(window):
        @pl.when(me - 1 - slot < 0)
        def _(slot=slot):
            seg_buf[slot] = jnp.zeros(seg_buf.shape[1:], seg_buf.dtype)
            for head in range(kv_heads):
                k_buf[head, slot * rows : (slot + 1) * rows] = jnp.zeros((rows, HEAD), k_buf.dtype)
                v_buf[head, slot * rows : (slot + 1) * rows] = jnp.zeros((rows, HEAD), v_buf.dtype)

    loads[1].wait()
    seg_own[...] = jnp.zeros_like(seg_own)
    seg_own[:, :rows] = seg_ref[...]
    lane = lax.broadcasted_iota(jnp.int32, (1, HEAD), 1)
    step = lax.rem(lane, HEAD // 2).astype(jnp.float32)
    frequency = jnp.exp(step * (-2.0 * math.log(1000000.0) / HEAD))
    position = me * rows + lax.broadcasted_iota(jnp.int32, (rows, 1), 0)
    angles = position.astype(jnp.float32) * frequency
    cosine = jnp.cos(angles)
    sine = jnp.where(lane < HEAD // 2, -1.0, 1.0) * jnp.sin(angles)

    def rotated(entries):
        wide = entries.astype(jnp.float32)
        return (wide * cosine + pltpu.roll(wide, HEAD // 2, 1) * sine).astype(jnp.bfloat16)

    loads[2].wait()
    for head in range(kv_heads):
        k_own[head] = rotated(k_ref[:, head * HEAD : (head + 1) * HEAD])
    loads[0].wait()

    pl.semaphore_wait(
        barrier, ways + (me + ways < n).astype(jnp.int32) + (me >= ways).astype(jnp.int32)
    )

    for chunk in range(chunks):
        send(-1, chunk)

    loads[3].wait()
    for head in range(q_heads):
        q_rot[head] = rotated(q_in[:, head * HEAD : (head + 1) * HEAD])

    loads[5].wait()
    valid = valid_ref[0]
    row_at = lax.broadcasted_iota(jnp.int32, (rows, rows), 0)
    col_at = lax.broadcasted_iota(jnp.int32, (rows, rows), 1)
    seg_row = seg_ref[...]
    seg_col = jnp.sum(jnp.where(row_at == col_at, seg_row, 0), axis=1, keepdims=True)
    ones = jnp.ones((2 * rows, HEAD), jnp.bfloat16)

    def attend(head0, count, keys, values, bias, before, total):
        width = keys.shape[0]
        tiles = -(-width // LANES)
        held = jnp.concatenate([values, ones[:width]], axis=1)
        results = []
        for part in range(0, count, BATCH):
            q = q_rot[pl.ds(head0 + part, BATCH)].reshape(BATCH * rows, HEAD)
            s = lax.dot_general(
                q, keys, (((1,), (1,)), ((), ())), preferred_element_type=jnp.float32
            )
            for i in range(BATCH):
                for r in range(0, rows, PART):
                    t = s[i * rows + r : i * rows + r + PART] * SCALE + bias[r : r + PART]
                    top = jnp.broadcast_to(jnp.max(t, axis=1, keepdims=True), (PART, LANES))
                    if before is not None:
                        old = before[head0 + part + i, r : r + PART]
                        top = jnp.maximum(top, old)
                    wide = jnp.concatenate([top] * tiles, axis=1)[:, :width]
                    p = jnp.exp2(t - wide).astype(jnp.bfloat16)
                    mixed = jnp.dot(p, held, preferred_element_type=jnp.float32)
                    if before is not None:
                        alpha = jnp.exp2(old - top)
                        mixed += total[head0 + part + i, r : r + PART] * jnp.concatenate([alpha, alpha], axis=1)
                    results.append((part + i, r, top, mixed))
        return results

    causal = (seg_row == seg_col) & (col_at <= row_at)
    causal = causal & ((me * rows + col_at < valid) | (col_at == row_at))
    bias_ref[:, :rows] = jnp.where(causal, 0.0, BLOCKED)
    per_step = min(4, group)

    def keep(head0, results):
        for i, r, top, mixed in results:
            acc_ref[head0 + i, r : r + PART] = mixed
            max_ref[head0 + i, r : r + PART] = top

    lead = ways - 1
    polls = [(0,), (1,), (2,), ()]
    for kv in range(kv_heads):
        for step in range(group // per_step):
            here = kv * group + step * per_step
            values = v_ref[:, kv * HEAD : (kv + 1) * HEAD]
            keep(here, attend(here, per_step, k_own[kv], values, bias_ref[:, :rows], None, None))
            for chunk in polls.pop(0) if polls else ():
                arrive(lead, chunk)

    def later(stage, kv, step, last):
        span = pl.ds(2 * stage * rows, 2 * rows)
        head0 = kv * group + step * per_step
        results = attend(head0, per_step, k_buf[kv, span], v_buf[kv, span], bias_ref[...], max_ref, acc_ref)
        if not last:
            keep(head0, results)
            return
        for i, r, top, mixed in results:
            out = mixed[:, :HEAD] / mixed[:, HEAD:]
            out = jnp.where(position[r : r + PART] < valid, out, 0.0)
            rew_acc[r : r + PART] += out * weight_ref[pl.ds(head0 + i, 1), :]
            out_buf[r : r + PART, pl.ds((head0 + i) * HEAD, HEAD)] = out.astype(jnp.bfloat16)

    loads[4].wait()
    rew_acc[...] = jnp.zeros_like(rew_acc)
    stages = window // 2
    lane_at = lax.broadcasted_iota(jnp.int32, (1, 2 * rows), 1)
    stores = []
    second = (lane_at >= rows).astype(jnp.int32)
    for stage in range(stages):
        near, far = 2 * stage, 2 * stage + 1
        order = (far, near) if ways == 2 else (near, far)
        for slot in order:
            arrive(slot, 0)
        seg_keys = jnp.concatenate([seg_buf[near][:, :rows], seg_buf[far][:, :rows]], axis=1)
        key_pos = (me - 1 - near - second) * rows + lane_at - second * rows
        allowed = (seg_keys == seg_col) & (key_pos >= 0) & (key_pos < valid)
        bias_ref[...] = jnp.where(allowed, 0.0, BLOCKED)
        last = stage == stages - 1
        for kv in range(kv_heads):
            for slot in order:
                arrive(slot, 1 + 2 * kv)
                arrive(slot, 2 + 2 * kv)
            steps = group // per_step
            for step in range(steps):
                later(stage, kv, step, last)
                if last:
                    head0 = kv * group + step * per_step
                    columns = pl.ds(head0 * HEAD, per_step * HEAD)
                    stores.append(
                        pltpu.make_async_copy(
                            out_buf.at[:, columns], out_hbm.at[:, columns], store_sem.at[head0 // per_step]
                        )
                    )
                    stores[-1].start()
                ahead = 2 * stage + lead + (0 if kv + 1 < kv_heads else 2)
                after = 1 + 2 * (kv + 1) if kv + 1 < kv_heads else 1
                if ahead > 2 * stage + 1:
                    arrive(ahead, 0)
                if step < 2:
                    arrive(ahead, after + step)

    mine = jnp.sum(rew_acc[...], axis=1, keepdims=True)
    mine_row = jnp.sum(jnp.where(row_at == col_at, mine, 0.0), axis=0, keepdims=True)
    rew_own[...] = jnp.zeros_like(rew_own)
    rew_own[:, :rows] = mine_row
    swap = pltpu.make_async_remote_copy(
        src_ref=rew_own,
        dst_ref=rew_far,
        send_sem=rew_sem.at[0],
        recv_sem=rew_sem.at[1],
        device_id={"tp": other},
        device_id_type=MESH,
    )
    swap.start()
    for slot in range(-1, window):
        for chunk in range(chunks):
            finish_send(slot, chunk)
    swap.wait()
    reward_ref[...] = mine_row + rew_far[:, :rows]
    for store in stores:
        store.wait()


def hand_over(out_near, rew_near, out_far, rew_far, out_stage, rew_stage, load_sem, store_sem):
    size = out_near.shape[0] // COPIES
    moves = [(rew_near, rew_stage, rew_far)]
    for at in range(COPIES):
        span = pl.ds(at * size, size)
        moves.append((out_near.at[span], out_stage.at[span], out_far.at[span]))
    loads = [
        pltpu.make_async_copy(near, stage, load_sem.at[at]) for at, (near, stage, far) in enumerate(moves)
    ]
    stores = [
        pltpu.make_async_copy(stage, far, store_sem.at[at]) for at, (near, stage, far) in enumerate(moves)
    ]
    for load in loads:
        load.start()
    for load, store in zip(loads, stores):
        load.wait()
        store.start()
    for store in stores:
        store.wait()


def per_device(n, queries, keys, values, segments, valid_length, reward_weight):
    rows = queries.shape[0]
    q_heads = queries.shape[1] // HEAD
    kv_heads = keys.shape[1] // HEAD
    span = rows * n // 2
    window = -(-(span - 1) // rows)
    window += window % 2
    ways = 2 if n <= 8 else 1
    chunks = 1 + 2 * kv_heads * PIECES
    wide = -(-rows // LANES) * LANES
    vmem = pl.BlockSpec(memory_space=pltpu.VMEM)
    hbm = pl.BlockSpec(memory_space=pltpu.HBM)
    attention, reward = pl.pallas_call(
        functools.partial(kernel, n, window, ways),
        out_shape=(
            jax.ShapeDtypeStruct(queries.shape, jnp.bfloat16),
            jax.ShapeDtypeStruct((1, rows), jnp.float32),
        ),
        in_specs=[
            hbm,
            hbm,
            hbm,
            hbm,
            hbm,
            hbm,
        ],
        out_specs=(hbm, vmem),
        scratch_shapes=[
            pltpu.VMEM(queries.shape, jnp.bfloat16),
            pltpu.VMEM(keys.shape, jnp.bfloat16),
            pltpu.VMEM(values.shape, jnp.bfloat16),
            pltpu.VMEM((1, rows), jnp.int32),
            pltpu.VMEM((q_heads, HEAD), jnp.float32),
            pltpu.SMEM((1,), jnp.int32),
            pltpu.VMEM((q_heads, rows, HEAD), jnp.bfloat16),
            pltpu.VMEM((kv_heads, rows, HEAD), jnp.bfloat16),
            pltpu.VMEM((kv_heads, window * rows, HEAD), jnp.bfloat16),
            pltpu.VMEM((kv_heads, window * rows, HEAD), jnp.bfloat16),
            pltpu.VMEM((1, wide), jnp.int32),
            pltpu.VMEM((window, 1, wide), jnp.int32),
            pltpu.VMEM((rows, 2 * rows), jnp.float32),
            pltpu.VMEM((q_heads, rows, LANES), jnp.float32),
            pltpu.VMEM((q_heads, rows, 2 * HEAD), jnp.float32),
            pltpu.VMEM(queries.shape, jnp.bfloat16),
            pltpu.VMEM((rows, HEAD), jnp.float32),
            pltpu.VMEM((1, wide), jnp.float32),
            pltpu.VMEM((1, wide), jnp.float32),
            pltpu.SemaphoreType.DMA((3, window, chunks)),
            pltpu.SemaphoreType.DMA((window, chunks)),
            pltpu.SemaphoreType.DMA((2,)),
            pltpu.SemaphoreType.DMA((6,)),
            pltpu.SemaphoreType.DMA((q_heads // 4,)),
        ],
        compiler_params=pltpu.CompilerParams(
            collective_id=0, has_side_effects=True, vmem_limit_bytes=60 * 1024 * 1024
        ),
    )(
        queries,
        keys,
        values,
        segments.reshape(1, rows),
        valid_length,
        reward_weight.reshape(q_heads, HEAD),
    )
    attention, reward = pl.pallas_call(
        hand_over,
        out_shape=(
            jax.ShapeDtypeStruct(queries.shape, jnp.bfloat16),
            jax.ShapeDtypeStruct((1, rows), jnp.float32),
        ),
        in_specs=[hbm, hbm],
        out_specs=(hbm, hbm),
        scratch_shapes=[
            pltpu.VMEM(queries.shape, jnp.bfloat16),
            pltpu.VMEM((1, rows), jnp.float32),
            pltpu.SemaphoreType.DMA((COPIES + 1,)),
            pltpu.SemaphoreType.DMA((COPIES + 1,)),
        ],
        compiler_params=pltpu.CompilerParams(vmem_limit_bytes=60 * 1024 * 1024),
    )(attention, reward)
    return attention, reward.reshape(rows)


def solution(mesh):
    return jax.shard_map(
        functools.partial(per_device, mesh.shape["ctx"]),
        mesh=mesh,
        in_specs=(
            P(("groups", "ctx"), "tp"),
            P(("groups", "ctx"), "tp"),
            P(("groups", "ctx"), "tp"),
            P(("groups", "ctx")),
            P("groups"),
            P("tp"),
        ),
        out_specs=(P(("groups", "ctx"), "tp"), P(("groups", "ctx"))),
        check_vma=False,
    )
```

```python
import functools
import math

import jax
import jax.numpy as jnp
from jax import lax
from jax.experimental import pallas as pl
from jax.experimental.pallas import tpu as pltpu
from jax.sharding import PartitionSpec as P

HEAD = 128
LANES = 128
MESH = pl.DeviceIdType.MESH
SCALE = HEAD**-0.5 * math.log2(math.e)
BLOCKED = -1e30
BATCH = 8
PART = 96
PIECES = 1
COPIES = 4


def kernel(
    n,
    window,
    ways,
    q_hbm,
    k_hbm,
    v_hbm,
    seg_hbm,
    valid_hbm,
    weight_hbm,
    out_hbm,
    reward_ref,
    q_in,
    k_ref,
    v_ref,
    seg_ref,
    weight_ref,
    valid_ref,
    q_rot,
    k_own,
    k_buf,
    v_buf,
    seg_own,
    seg_buf,
    bias_ref,
    max_ref,
    acc_ref,
    out_buf,
    rew_acc,
    rew_own,
    rew_far,
    send_sem,
    recv_sem,
    rew_sem,
    load_sem,
    store_sem,
):
    rows = k_ref.shape[0]
    kv_heads = k_ref.shape[1] // HEAD
    q_heads = q_in.shape[1] // HEAD
    group = q_heads // kv_heads
    chunks = 1 + 2 * kv_heads * PIECES
    me = lax.axis_index("ctx")
    other = 1 - lax.axis_index("tp")
    odd = lax.rem(me, 2)

    barrier = pltpu.get_barrier_semaphore()
    pl.semaphore_signal(barrier, inc=1, device_id={"tp": other}, device_id_type=MESH)
    if ways == 2:
        pl.semaphore_signal(barrier, inc=1, device_id={"ctx": me + 1 - 2 * odd}, device_id_type=MESH)

    @pl.when(me + ways < n)
    def _():
        pl.semaphore_signal(barrier, inc=1, device_id={"ctx": me + ways}, device_id_type=MESH)

    @pl.when(me >= ways)
    def _():
        pl.semaphore_signal(barrier, inc=1, device_id={"ctx": me - ways}, device_id_type=MESH)

    loads = []
    pairs = ((v_hbm, v_ref), (seg_hbm, seg_ref), (k_hbm, k_ref), (q_hbm, q_in), (weight_hbm, weight_ref), (valid_hbm, valid_ref))
    for at, (source, target) in enumerate(pairs):
        loads.append(pltpu.make_async_copy(source, target, load_sem.at[at]))
        loads[-1].start()

    def outgoing(slot, chunk):
        held = me - 1 - slot >= 0
        if ways == 1:
            return [(0, slot + 1, me + 1, held & (me + 1 < n))] if slot + 1 < window else []
        sends = []
        late = chunk == chunks - 1
        if slot == -1 or slot % 2 == 1:
            if slot + 2 < window:
                sends.append((0, slot + 2, me + 2, held & (me + 2 < n)))
            if slot + 1 < window:
                sends.append((1, slot + 1, me + 1, held & (odd == 0)))
            if slot == 1 or (slot > 1 and not late):
                sends.append((2, slot - 1, me - 1, held & (odd == 1)))
        elif late and slot + 2 < window:
            sends.append((2, slot + 2, me + 2, held & (odd == 0) & (me + 2 < n)))
        return sends

    def piece(slot, chunk):
        if chunk == 0:
            return seg_own if slot < 0 else seg_buf.at[slot]
        which, part = (chunk - 1) // PIECES, (chunk - 1) % PIECES
        head, is_key = which // 2, which % 2 == 1
        size = rows // PIECES
        if slot < 0:
            own = pl.ds(part * size, size)
            return k_own.at[head, own] if is_key else v_ref.at[own, pl.ds(head * HEAD, HEAD)]
        return (k_buf if is_key else v_buf).at[head, pl.ds(slot * rows + part * size, size)]

    def copy_of(slot, chunk, path, there, device):
        return pltpu.make_async_remote_copy(
            src_ref=piece(slot, chunk),
            dst_ref=piece(there, chunk),
            send_sem=send_sem.at[path, there, chunk],
            recv_sem=recv_sem.at[there, chunk],
            device_id={"ctx": device},
            device_id_type=MESH,
        )

    def send(slot, chunk, paths=(0, 1, 2)):
        for path, there, device, condition in outgoing(slot, chunk):
            if path not in paths:
                continue

            @pl.when(condition)
            def _(path=path, there=there, device=device):
                copy_of(slot, chunk, path, there, device).start()

    def finish_send(slot, chunk):
        for path, there, device, condition in outgoing(slot, chunk):
            @pl.when(condition)
            def _(path=path, there=there, device=device):
                copy_of(slot, chunk, path, there, device).wait_send()

    arrived = set()

    def arrive(slot, which):
        if slot >= window or which > 2 * kv_heads or (slot, which) in arrived:
            return
        arrived.add((slot, which))
        for chunk in (0,) if which == 0 else range(1 + (which - 1) * PIECES, 1 + which * PIECES):
            @pl.when(me - 1 - slot >= 0)
            def _(chunk=chunk):
                copy_of(slot, chunk, 0, slot, me).wait_recv()

            send(slot, chunk)

    for slot in range(window):
        @pl.when(me - 1 - slot < 0)
        def _(slot=slot):
            seg_buf[slot] = jnp.zeros(seg_buf.shape[1:], seg_buf.dtype)
            for head in range(kv_heads):
                k_buf[head, slot * rows : (slot + 1) * rows] = jnp.zeros((rows, HEAD), k_buf.dtype)
                v_buf[head, slot * rows : (slot + 1) * rows] = jnp.zeros((rows, HEAD), v_buf.dtype)

    loads[1].wait()
    seg_own[...] = jnp.zeros_like(seg_own)
    seg_own[:, :rows] = seg_ref[...]
    lane = lax.broadcasted_iota(jnp.int32, (1, HEAD), 1)
    step = lax.rem(lane, HEAD // 2).astype(jnp.float32)
    frequency = jnp.exp(step * (-2.0 * math.log(1000000.0) / HEAD))
    position = me * rows + lax.broadcasted_iota(jnp.int32, (rows, 1), 0)
    angles = position.astype(jnp.float32) * frequency
    cosine = jnp.cos(angles)
    sine = jnp.where(lane < HEAD // 2, -1.0, 1.0) * jnp.sin(angles)

    def rotated(entries):
        wide = entries.astype(jnp.float32)
        return (wide * cosine + pltpu.roll(wide, HEAD // 2, 1) * sine).astype(jnp.bfloat16)

    loads[2].wait()
    for head in range(kv_heads):
        k_own[head] = rotated(k_ref[:, head * HEAD : (head + 1) * HEAD])
    loads[0].wait()

    pl.semaphore_wait(
        barrier, ways + (me + ways < n).astype(jnp.int32) + (me >= ways).astype(jnp.int32)
    )

    for path in range(2):
        for chunk in range(chunks):
            send(-1, chunk, (path,))

    loads[3].wait()
    for head in range(q_heads):
        q_rot[head] = rotated(q_in[:, head * HEAD : (head + 1) * HEAD])

    loads[5].wait()
    valid = valid_ref[0]
    row_at = lax.broadcasted_iota(jnp.int32, (rows, rows), 0)
    col_at = lax.broadcasted_iota(jnp.int32, (rows, rows), 1)
    seg_row = seg_ref[...]
    seg_col = jnp.sum(jnp.where(row_at == col_at, seg_row, 0), axis=1, keepdims=True)
    ones = jnp.ones((2 * rows, HEAD), jnp.bfloat16)

    def attend(head0, count, keys, values, bias, before, total):
        width = keys.shape[0]
        tiles = -(-width // LANES)
        held = jnp.concatenate([values, ones[:width]], axis=1)
        results = []
        for part in range(0, count, BATCH):
            q = q_rot[pl.ds(head0 + part, BATCH)].reshape(BATCH * rows, HEAD)
            s = lax.dot_general(
                q, keys, (((1,), (1,)), ((), ())), preferred_element_type=jnp.float32
            )
            for i in range(BATCH):
                for r in range(0, rows, PART):
                    t = s[i * rows + r : i * rows + r + PART] * SCALE + bias[r : r + PART]
                    top = jnp.broadcast_to(jnp.max(t, axis=1, keepdims=True), (PART, LANES))
                    if before is not None:
                        old = before[head0 + part + i, r : r + PART]
                        top = jnp.maximum(top, old)
                    wide = jnp.concatenate([top] * tiles, axis=1)[:, :width]
                    p = jnp.exp2(t - wide).astype(jnp.bfloat16)
                    mixed = jnp.dot(p, held, preferred_element_type=jnp.float32)
                    if before is not None:
                        alpha = jnp.exp2(old - top)
                        mixed += total[head0 + part + i, r : r + PART] * jnp.concatenate([alpha, alpha], axis=1)
                    results.append((part + i, r, top, mixed))
        return results

    causal = (seg_row == seg_col) & (col_at <= row_at)
    causal = causal & ((me * rows + col_at < valid) | (col_at == row_at))
    bias_ref[:, :rows] = jnp.where(causal, 0.0, BLOCKED)
    per_step = min(8, group)

    def keep(head0, results):
        for i, r, top, mixed in results:
            acc_ref[head0 + i, r : r + PART] = mixed
            max_ref[head0 + i, r : r + PART] = top

    lead = ways - 1
    polls = [(), (0, 1)]
    for kv in range(kv_heads):
        for step in range(group // per_step):
            here = kv * group + step * per_step
            values = v_ref[:, kv * HEAD : (kv + 1) * HEAD]
            keep(here, attend(here, per_step, k_own[kv], values, bias_ref[:, :rows], None, None))
            for chunk in polls.pop(0) if polls else ():
                arrive(lead, chunk)

    def later(stage, kv, step, last):
        span = pl.ds(2 * stage * rows, 2 * rows)
        head0 = kv * group + step * per_step
        results = attend(head0, per_step, k_buf[kv, span], v_buf[kv, span], bias_ref[...], max_ref, acc_ref)
        if not last:
            keep(head0, results)
            return
        for i, r, top, mixed in results:
            out = mixed[:, :HEAD] / mixed[:, HEAD:]
            out = jnp.where(position[r : r + PART] < valid, out, 0.0)
            rew_acc[r : r + PART] += out * weight_ref[pl.ds(head0 + i, 1), :]
            out_buf[r : r + PART, pl.ds((head0 + i) * HEAD, HEAD)] = out.astype(jnp.bfloat16)

    loads[4].wait()
    rew_acc[...] = jnp.zeros_like(rew_acc)
    stages = window // 2
    lane_at = lax.broadcasted_iota(jnp.int32, (1, 2 * rows), 1)
    stores = []
    second = (lane_at >= rows).astype(jnp.int32)
    for stage in range(stages):
        near, far = 2 * stage, 2 * stage + 1
        order = (far, near) if ways == 2 else (near, far)
        for slot in order:
            arrive(slot, 0)
        seg_keys = jnp.concatenate([seg_buf[near][:, :rows], seg_buf[far][:, :rows]], axis=1)
        key_pos = (me - 1 - near - second) * rows + lane_at - second * rows
        allowed = (seg_keys == seg_col) & (key_pos >= 0) & (key_pos < valid)
        bias_ref[...] = jnp.where(allowed, 0.0, BLOCKED)
        last = stage == stages - 1
        for kv in range(kv_heads):
            for slot in order:
                arrive(slot, 1 + 2 * kv)
                arrive(slot, 2 + 2 * kv)
            steps = group // per_step
            for step in range(steps):
                later(stage, kv, step, last)
                if last:
                    head0 = kv * group + step * per_step
                    columns = pl.ds(head0 * HEAD, per_step * HEAD)
                    stores.append(
                        pltpu.make_async_copy(
                            out_buf.at[:, columns], out_hbm.at[:, columns], store_sem.at[head0 // per_step]
                        )
                    )
                    stores[-1].start()
                ahead = 2 * stage + lead + (0 if kv + 1 < kv_heads else 2)
                after = 1 + 2 * (kv + 1) if kv + 1 < kv_heads else 1
                if ahead > 2 * stage + 1:
                    arrive(ahead, 0)
                if step < 2:
                    arrive(ahead, after + step)

    mine = jnp.sum(rew_acc[...], axis=1, keepdims=True)
    mine_row = jnp.sum(jnp.where(row_at == col_at, mine, 0.0), axis=0, keepdims=True)
    rew_own[...] = jnp.zeros_like(rew_own)
    rew_own[:, :rows] = mine_row
    swap = pltpu.make_async_remote_copy(
        src_ref=rew_own,
        dst_ref=rew_far,
        send_sem=rew_sem.at[0],
        recv_sem=rew_sem.at[1],
        device_id={"tp": other},
        device_id_type=MESH,
    )
    swap.start()
    for slot in range(-1, window):
        for chunk in range(chunks):
            finish_send(slot, chunk)
    swap.wait()
    reward_ref[...] = mine_row + rew_far[:, :rows]
    for store in stores:
        store.wait()


def hand_over(out_near, rew_near, out_far, rew_far, out_stage, rew_stage, load_sem, store_sem):
    size = out_near.shape[0] // COPIES
    moves = [(rew_near, rew_stage, rew_far)]
    for at in range(COPIES):
        span = pl.ds(at * size, size)
        moves.append((out_near.at[span], out_stage.at[span], out_far.at[span]))
    loads = [
        pltpu.make_async_copy(near, stage, load_sem.at[at]) for at, (near, stage, far) in enumerate(moves)
    ]
    stores = [
        pltpu.make_async_copy(stage, far, store_sem.at[at]) for at, (near, stage, far) in enumerate(moves)
    ]
    for load in loads:
        load.start()
    for load, store in zip(loads, stores):
        load.wait()
        store.start()
    for store in stores:
        store.wait()


def per_device(n, queries, keys, values, segments, valid_length, reward_weight):
    rows = queries.shape[0]
    q_heads = queries.shape[1] // HEAD
    kv_heads = keys.shape[1] // HEAD
    span = rows * n // 2
    window = -(-(span - 1) // rows)
    window += window % 2
    ways = 2 if n <= 8 else 1
    chunks = 1 + 2 * kv_heads * PIECES
    wide = -(-rows // LANES) * LANES
    vmem = pl.BlockSpec(memory_space=pltpu.VMEM)
    hbm = pl.BlockSpec(memory_space=pltpu.HBM)
    attention, reward = pl.pallas_call(
        functools.partial(kernel, n, window, ways),
        out_shape=(
            jax.ShapeDtypeStruct(queries.shape, jnp.bfloat16),
            jax.ShapeDtypeStruct((1, rows), jnp.float32),
        ),
        in_specs=[
            hbm,
            hbm,
            hbm,
            hbm,
            hbm,
            hbm,
        ],
        out_specs=(hbm, vmem),
        scratch_shapes=[
            pltpu.VMEM(queries.shape, jnp.bfloat16),
            pltpu.VMEM(keys.shape, jnp.bfloat16),
            pltpu.VMEM(values.shape, jnp.bfloat16),
            pltpu.VMEM((1, rows), jnp.int32),
            pltpu.VMEM((q_heads, HEAD), jnp.float32),
            pltpu.SMEM((1,), jnp.int32),
            pltpu.VMEM((q_heads, rows, HEAD), jnp.bfloat16),
            pltpu.VMEM((kv_heads, rows, HEAD), jnp.bfloat16),
            pltpu.VMEM((kv_heads, window * rows, HEAD), jnp.bfloat16),
            pltpu.VMEM((kv_heads, window * rows, HEAD), jnp.bfloat16),
            pltpu.VMEM((1, wide), jnp.int32),
            pltpu.VMEM((window, 1, wide), jnp.int32),
            pltpu.VMEM((rows, 2 * rows), jnp.float32),
            pltpu.VMEM((q_heads, rows, LANES), jnp.float32),
            pltpu.VMEM((q_heads, rows, 2 * HEAD), jnp.float32),
            pltpu.VMEM(queries.shape, jnp.bfloat16),
            pltpu.VMEM((rows, HEAD), jnp.float32),
            pltpu.VMEM((1, wide), jnp.float32),
            pltpu.VMEM((1, wide), jnp.float32),
            pltpu.SemaphoreType.DMA((3, window, chunks)),
            pltpu.SemaphoreType.DMA((window, chunks)),
            pltpu.SemaphoreType.DMA((2,)),
            pltpu.SemaphoreType.DMA((6,)),
            pltpu.SemaphoreType.DMA((q_heads // 8,)),
        ],
        compiler_params=pltpu.CompilerParams(
            collective_id=0, has_side_effects=True, vmem_limit_bytes=60 * 1024 * 1024
        ),
    )(
        queries,
        keys,
        values,
        segments.reshape(1, rows),
        valid_length,
        reward_weight.reshape(q_heads, HEAD),
    )
    attention, reward = pl.pallas_call(
        hand_over,
        out_shape=(
            jax.ShapeDtypeStruct(queries.shape, jnp.bfloat16),
            jax.ShapeDtypeStruct((1, rows), jnp.float32),
        ),
        in_specs=[hbm, hbm],
        out_specs=(hbm, hbm),
        scratch_shapes=[
            pltpu.VMEM(queries.shape, jnp.bfloat16),
            pltpu.VMEM((1, rows), jnp.float32),
            pltpu.SemaphoreType.DMA((COPIES + 1,)),
            pltpu.SemaphoreType.DMA((COPIES + 1,)),
        ],
        compiler_params=pltpu.CompilerParams(vmem_limit_bytes=60 * 1024 * 1024),
    )(attention, reward)
    return attention, reward.reshape(rows)


def solution(mesh):
    return jax.shard_map(
        functools.partial(per_device, mesh.shape["ctx"]),
        mesh=mesh,
        in_specs=(
            P(("groups", "ctx"), "tp"),
            P(("groups", "ctx"), "tp"),
            P(("groups", "ctx"), "tp"),
            P(("groups", "ctx")),
            P("groups"),
            P("tp"),
        ),
        out_specs=(P(("groups", "ctx"), "tp"), P(("groups", "ctx"))),
        check_vma=False,
    )
```
